32 devices in a mesh: groups: 2 (over y), gx: 4 (over z), gy: 2 (over x), gz: 2 (over core).
Axes of the slice: x: 2, y: 2, z: 4, core: 2. Of those that a mesh axis runs over, the one named last changes fastest.
Arguments:
- tokens: bfloat16 [192, 8192], P(('groups', 'gx', 'gy'), 'gz'), parts along dimension 0, may hold values from -6 to 6
- gate_weight: bfloat16 [8192, 14336], P('gz', ('gx', 'gy')), may hold values from -0.0625 to 0.0625
- up_weight: bfloat16 [8192, 14336], P('gz', ('gx', 'gy')), may hold values from -0.0625 to 0.0625
- down_weight: bfloat16 [14336, 8192], P('gx', ('gy', 'gz')), may hold values from -0.046875 to 0.046875
- reward_weight: bfloat16 [8192], P(('gy', 'gz')), may hold values from -0.0625 to 0.0625
- candidate_ids: int32 [192], P('groups'), parts along dimension 0, may hold values from 0 to 15, never falling along the last dimension, each value on 1 to 12 neighbouring positions
Outputs:
- mixed: bfloat16 [192, 8192], P(('groups', 'gx'), ('gy', 'gz')), parts along dimension 0
- scores: float32 [32], P('groups'), parts along dimension 0
The draws below stay inside these ranges and needn't reach their ends.
There are 2 independent parts, one for each index of `groups`. The reference program is written for one: setup_inputs(seed, part) draws one part's arguments, and reference() takes and returns one part's arrays. A program takes and returns all parts, laid end to end along the dimension named above; an argument that names none is the same for every part. Nothing has to cross between parts.
Inputs may be any that keep to these rules, and one draw needn't show every extreme that they name: `candidate_ids`: numbers never fall along the tokens; every candidate has 1 to 12 consecutive tokens, one exactly 12.
All inputs are finite; a program needn't handle non-finite values.
Results may differ from the reference program's by a relative error of at most 0.03.
Values may be sent and summed in bfloat16 or wider, within the bound.
A program may use at most 128 MiB of HBM per device.

```python
import math
import jax
import jax.numpy as jnp
import numpy as np
from jax import lax

D = 8192
FF = 14336
CANDS = 16
TOKENS = 96
N_GX = 4
N_GZ = 2


def shard_levels(stream_key, extent, split, least, top_value):
    factor_of, own = 1.0, jax.random.fold_in(stream_key, 6)
    for dim, blocks in split:
        steps = jnp.exp(jax.random.uniform(jax.random.fold_in(own, dim), (blocks,), jnp.float32, least / len(split), top_value / len(split)))
        factor_of = factor_of * jnp.repeat(steps, extent[dim] // blocks).reshape([-1 if axis == dim else 1 for axis in range(len(extent))])
    return factor_of


def length_profile(number_of, total, limit, skew):
    loads = [(1 << 20) // math.isqrt(standing ** skew) + 1 for standing in range(2, number_of + 1)]
    surplus, given = total - limit - (number_of - 1), [1] * (number_of - 1)
    while surplus > 0:
        candidates = [i for i in range(number_of - 1) if given[i] < limit]
        whole, left = sum([loads[i] for i in candidates]), surplus
        for i in candidates:
            more = min(limit - given[i], max(1, left * loads[i] // whole), surplus)
            given[i] = given[i] + more
            surplus = surplus - more
    return np.array([limit] + given)


def ragged(rng, number_of, total, reach, slope):
    if number_of == 2:
        one = jax.random.randint(rng, (), max(1, total - reach), min(reach, total - 1) + 1)
        return jnp.stack([one, total - one])
    sizes = jnp.asarray(length_profile(number_of, total, reach, slope), jnp.int32)
    couples = (number_of - 1) // 2
    source_of, sink = sizes[1:1 + 2 * couples:2], sizes[2:2 + 2 * couples:2]
    room = jnp.minimum(source_of - 1, reach - sink)
    moved = jax.random.randint(jax.random.fold_in(rng, 1), (couples,), 0, 1 << 20) % (room + 1)
    sizes = sizes.at[1:1 + 2 * couples:2].set(source_of - moved).at[2:2 + 2 * couples:2].set(sink + moved)
    return sizes[jax.random.permutation(jax.random.fold_in(rng, 2), number_of)]


def noise(own_key, dims, width, reach, pieces=(), kind=jnp.bfloat16):
    loudness = shard_levels(own_key, dims, pieces, -0.22, 0.18) if pieces else 1.0
    values = jax.random.normal(own_key, dims, jnp.float32) * width * loudness
    return jnp.minimum(jnp.maximum(values, -reach), reach).astype(kind)


def setup_inputs(seed: int = 0, part: int = 0) -> dict:
    keys = jax.random.split(jax.random.key(seed), 7)
    part_splits = jax.random.split(jax.random.fold_in(keys[6], part), 7)
    tokens = noise(part_splits[0], (TOKENS, D), 1.0, 6.0, ((0, 8), (1, 2)))
    gate_weight = noise(keys[1], (D, FF), D ** -0.5, 0.0625, ((0, 2), (1, 8)))
    up_weight = noise(keys[2], (D, FF), D ** -0.5, 0.0625, ((0, 2), (1, 8)))
    down_weight = noise(keys[3], (FF, D), FF ** -0.5, 0.046875, ((0, 4), (1, 4)))
    reward_weight = noise(keys[4], (D,), D ** -0.5, 0.0625, ((0, 4),))
    candidate_ids = jnp.searchsorted(jnp.cumsum(ragged(part_splits[5], CANDS, TOKENS, TOKENS // 8, 1)), jnp.arange(TOKENS), side="right").astype(jnp.int32)
    return dict(tokens=tokens, gate_weight=gate_weight, up_weight=up_weight, down_weight=down_weight, reward_weight=reward_weight, candidate_ids=candidate_ids)


def rounded(value):
    return lax.optimization_barrier(value.astype(jnp.bfloat16)).astype(jnp.float32)


def reference(tokens, gate_weight, up_weight, down_weight, reward_weight, candidate_ids):
    half_width = D // N_GZ
    gate = jnp.zeros((TOKENS, FF), jnp.float32)
    upper = jnp.zeros((TOKENS, FF), jnp.float32)
    for block in range(N_GZ):
        cols = tokens[:, block * half_width:(block + 1) * half_width]
        gate = gate + rounded(jnp.dot(cols, gate_weight[block * half_width:(block + 1) * half_width], preferred_element_type=jnp.float32))
        upper = upper + rounded(jnp.dot(cols, up_weight[block * half_width:(block + 1) * half_width], preferred_element_type=jnp.float32))
    hidden = (jax.nn.silu(gate) * upper).astype(jnp.bfloat16)
    unit_block = FF // N_GX
    total = jnp.zeros((TOKENS, D), jnp.float32)
    for block in range(N_GX):
        piece = jnp.dot(hidden[:, block * unit_block:(block + 1) * unit_block], down_weight[block * unit_block:(block + 1) * unit_block], preferred_element_type=jnp.float32)
        total = total + rounded(piece)
    mixed = total.astype(jnp.bfloat16)
    values = jnp.dot(mixed, reward_weight, preferred_element_type=jnp.float32)
    following = jnp.concatenate([candidate_ids[1:], jnp.full((1,), -1, jnp.int32)])
    is_last = candidate_ids != following
    matches = (candidate_ids[:, None] == jnp.arange(CANDS, dtype=jnp.int32)[None, :]) & is_last[:, None]
    scores = jnp.sum(jnp.where(matches, values[:, None], jnp.zeros_like(values)[:, None]), axis=0)
    return mixed, scores
```

```python
import jax
import jax.numpy as jnp
from jax import lax
from jax.experimental import pallas as pl
from jax.experimental.pallas import tpu as pltpu
from jax.sharding import PartitionSpec as P

CANDS = 16


def swiglu_pair(summed, unit_count):
    row_count = summed.shape[0]
    split_pair = summed.reshape(row_count, -1, 2, unit_count)
    gate_part = split_pair[:, :, 0, :].reshape(row_count, -1)
    upper_part = split_pair[:, :, 1, :].reshape(row_count, -1)
    return (jax.nn.silu(gate_part) * upper_part).astype(jnp.bfloat16)


def combine_pairs(partial_value, unit_count):
    summed = lax.psum(partial_value.astype(jnp.bfloat16), "gz").astype(jnp.float32)
    return swiglu_pair(summed, unit_count)


def plain_local(tokens, gate_weight, up_weight, down_weight, reward_weight, candidate_ids):
    unit_count = gate_weight.shape[1]
    paired = jnp.concatenate([gate_weight, up_weight], axis=1)
    local_rows = tokens.shape[0]
    gy_count = lax.axis_size("gy")
    out_rows = local_rows * gy_count
    all_tokens = lax.all_gather(tokens, ("gx", "gy"), axis=0, tiled=True)
    partial_value = jnp.dot(all_tokens, paired, preferred_element_type=jnp.float32)
    hidden_part = combine_pairs(partial_value, unit_count)
    hidden_all = lax.all_gather(hidden_part, "gy", axis=1, tiled=True)
    summed_out = lax.psum_scatter(
        jnp.dot(hidden_all, down_weight, preferred_element_type=jnp.float32).astype(jnp.bfloat16),
        "gx",
        scatter_dimension=0,
        tiled=True,
    )
    values = jnp.dot(summed_out, reward_weight, preferred_element_type=jnp.float32)
    first_row = lax.axis_index("gx") * out_rows
    extended = jnp.concatenate([candidate_ids, jnp.full((1,), -1, jnp.int32)])
    own_ids = lax.dynamic_slice_in_dim(extended, first_row, out_rows, 0)
    next_ids = lax.dynamic_slice_in_dim(extended, first_row + 1, out_rows, 0)
    matches = (own_ids[:, None] == jnp.arange(CANDS, dtype=jnp.int32)[None, :]) & (
        own_ids != next_ids
    )[:, None]
    partial_scores = jnp.sum(
        jnp.where(matches, values[:, None], jnp.zeros_like(values)[:, None]), axis=0
    )
    scores = lax.psum(partial_scores, ("gx", "gy", "gz"))
    return (summed_out, scores)


MESH = pl.DeviceIdType.MESH
WIDE = 256
OUT_WIDE = 512
VMEM_BYTES = 60 * 1024 * 1024


def fused_kernel(
    sizes, tok_ref, gate_ref, up_ref, down_ref, reward_ref, ids_ref, out_ref, score_ref,
    tok_f32, x_f32, x_bf, blocks, gate_buf, up_buf, down_buf, part, part_in, hid, term, term_in, score_buf,
    gate_sem, up_sem, down_sem, tok_send, tok_recv, part_send, part_recv, hid_send, hid_recv,
    term_send, term_recv, score_send, score_recv,
):
    nx, rows, pieces, chunks, out_chunks = sizes
    cut = tok_ref.shape[1] // pieces
    out_rows = 2 * rows
    total_rows = x_bf.shape[0]
    half = WIDE // 2
    out_half = OUT_WIDE // 2
    group, gx, gy, gz = (lax.axis_index(a) for a in ("groups", "gx", "gy", "gz"))
    gy_other, gz_other = 1 - gy, 1 - gz
    devices = nx * 4
    own = (gx * 2 + gy) * 2 + gz

    def peer(step):
        index = lax.rem(own + step, devices)
        return (group, index // 4, lax.rem(index // 2, 2), lax.rem(index, 2))

    def weight_copy(source, target, sem, c, width):
        return pltpu.make_async_copy(
            source.at[:, pl.ds(pl.multiple_of(c * width, width), width)], target.at[c], sem.at[c]
        )

    @pl.loop(0, chunks)
    def _(c):
        weight_copy(gate_ref, gate_buf, gate_sem, c, WIDE).start()
        weight_copy(up_ref, up_buf, up_sem, c, WIDE).start()

    @pl.loop(0, out_chunks)
    def _(c):
        weight_copy(down_ref, down_buf, down_sem, c, OUT_WIDE).start()

    barrier = pltpu.get_barrier_semaphore()

    @pl.loop(1, devices)
    def _(step):
        pl.semaphore_signal(barrier, inc=1, device_id=peer(step), device_id_type=MESH)

    mine = gx * 2 + gy
    for p in range(pieces):
        tok_f32[pl.ds(p * rows, rows), :] = tok_ref[:, pl.ds(p * cut, cut)].astype(jnp.float32)
    blocks[mine] = tok_f32[...].astype(jnp.bfloat16)
    pl.semaphore_wait(barrier, devices - 1)

    def tok_copy(slot, send, target):
        return pltpu.make_async_remote_copy(
            src_ref=blocks.at[slot], dst_ref=blocks.at[slot], send_sem=tok_send.at[send],
            recv_sem=tok_recv.at[slot], device_id=target, device_id_type=MESH,
        )

    @pl.loop(1, nx)
    def _(step):
        tok_copy(mine, step, (group, lax.rem(gx + step, nx), gy, gz)).start()

    x_peer = (group, gx, gy_other, gz)
    tok_copy(mine, 0, x_peer).start()

    @pl.loop(1, nx)
    def _(step):
        slot = lax.rem(gx + nx - step, nx) * 2 + gy
        tok_copy(slot, 0, x_peer).wait_recv()
        tok_copy(slot, nx + step, x_peer).start()

    @pl.loop(0, nx)
    def _(step):
        slot = lax.rem(gx + nx - step, nx) * 2 + gy_other
        tok_copy(slot, 0, x_peer).wait_recv()

    for d in range(nx * 2):
        tok_f32[...] = blocks[d].astype(jnp.float32)
        for p in range(pieces):
            x_f32[pl.ds(d * rows, rows), pl.ds(p * cut, cut)] = tok_f32[pl.ds(p * rows, rows), :]
    x_bf[...] = x_f32[...].astype(jnp.bfloat16)

    def part_copy(c):
        return pltpu.make_async_remote_copy(
            src_ref=part.at[c, gz_other], dst_ref=part_in.at[c], send_sem=part_send.at[c],
            recv_sem=part_recv.at[c], device_id=(group, gx, gy, gz_other), device_id_type=MESH,
        )

    def hid_block(c, y, z):
        return (y * chunks + c) * 2 + z

    def hid_copy(block, send, target):
        cols = hid.at[:, pl.ds(pl.multiple_of(block * half, half), half)]
        return pltpu.make_async_remote_copy(
            src_ref=cols, dst_ref=cols, send_sem=hid_send.at[send],
            recv_sem=hid_recv.at[block], device_id=target, device_id_type=MESH,
        )

    hid_targets = (
        (group, gx, gy_other, gz), (group, gx, gy_other, gz_other), (group, gx, gy, gz_other),
    )

    def finish(c):
        part_copy(c).wait_recv()
        gate = part[c, gz, pl.ds(0, total_rows), :].astype(jnp.float32) + part_in[c, pl.ds(0, total_rows), :].astype(jnp.float32)
        up = part[c, gz, pl.ds(total_rows, total_rows), :].astype(jnp.float32) + part_in[c, pl.ds(total_rows, total_rows), :].astype(jnp.float32)
        block = hid_block(c, gy, gz)
        hid[:, pl.ds(pl.multiple_of(block * half, half), half)] = (jax.nn.silu(gate) * up).astype(jnp.bfloat16)
        for n, target in enumerate(hid_targets):
            hid_copy(block, c * 3 + n, target).start()

    @pl.loop(0, chunks)
    def _(c):
        weight_copy(gate_ref, gate_buf, gate_sem, c, WIDE).wait()
        weight_copy(up_ref, up_buf, up_sem, c, WIDE).wait()
        x = x_bf[...]
        for n, weight in enumerate((gate_buf, up_buf)):
            product = jnp.dot(x, weight[c], preferred_element_type=jnp.float32).astype(jnp.bfloat16)
            for z in range(2):
                part[c, z, pl.ds(n * total_rows, total_rows), :] = product[:, z * half:(z + 1) * half]
        part_copy(c).start()

        @pl.when(c > 0)
        def _():
            finish(c - 1)

    finish(chunks - 1)

    @pl.loop(0, chunks)
    def _(c):
        hid_copy(hid_block(c, gy, gz_other), 0, x_peer).wait_recv()
        hid_copy(hid_block(c, gy_other, gz), 0, x_peer).wait_recv()
        hid_copy(hid_block(c, gy_other, gz_other), 0, x_peer).wait_recv()

    def term_copy(n, step):
        to = lax.rem(gx + step, nx)
        return pltpu.make_async_remote_copy(
            src_ref=term.at[n, to], dst_ref=term_in.at[n, gx], send_sem=term_send.at[n, step],
            recv_sem=term_recv.at[n, gx], device_id=(group, to, gy, gz), device_id_type=MESH,
        )

    def term_arrival(n, step):
        sender = lax.rem(gx + nx - step, nx)
        return sender, pltpu.make_async_remote_copy(
            src_ref=term.at[n, sender], dst_ref=term_in.at[n, sender], send_sem=term_send.at[n, step],
            recv_sem=term_recv.at[n, sender], device_id=(group, sender, gy, gz), device_id_type=MESH,
        )

    @pl.loop(0, out_chunks)
    def _(n):
        weight_copy(down_ref, down_buf, down_sem, n, OUT_WIDE).wait()
        product = jnp.dot(hid[...], down_buf[n], preferred_element_type=jnp.float32)
        for to in range(nx):
            block = product[to * out_rows:(to + 1) * out_rows, :]
            term[n, to] = jnp.concatenate([block[:, :out_half], block[:, out_half:]], axis=0).astype(jnp.bfloat16)

        @pl.loop(1, nx)
        def _(step):
            term_copy(n, step).start()

    values = jnp.zeros((out_rows, 1), jnp.float32)
    for n in range(out_chunks):
        summed = term[n, gx].astype(jnp.float32)
        for step in range(1, nx):
            sender, arrival = term_arrival(n, step)
            arrival.wait_recv()
            summed = summed + term_in[n, sender].astype(jnp.float32)
        for h in range(2):
            cols = pl.ds(n * OUT_WIDE + h * out_half, out_half)
            mixed = summed[h * out_rows:(h + 1) * out_rows, :].astype(jnp.bfloat16)
            out_ref[:, cols] = mixed
            values = values + jnp.sum(mixed.astype(jnp.float32) * reward_ref[:, cols], axis=1, keepdims=True)

    spread = jnp.concatenate([jnp.where(gx == j, values, jnp.zeros_like(values)) for j in range(nx)], axis=0)
    spread = jnp.broadcast_to(spread, (total_rows, 128))
    matches = (ids_ref[...] == lax.broadcasted_iota(jnp.int32, (CANDS, total_rows), 0)).astype(jnp.float32)
    score_buf[own] = jnp.dot(matches, spread, preferred_element_type=jnp.float32, precision=lax.Precision.HIGHEST)

    def score_copy(slot, step):
        return pltpu.make_async_remote_copy(
            src_ref=score_buf.at[slot], dst_ref=score_buf.at[slot], send_sem=score_send.at[step],
            recv_sem=score_recv.at[slot], device_id=peer(step), device_id_type=MESH,
        )

    @pl.loop(1, devices)
    def _(step):
        score_copy(own, step).start()

    @pl.loop(0, nx)
    def _(step):
        tok_copy(mine, step, x_peer).wait_send()

    @pl.loop(1, nx)
    def _(step):
        tok_copy(mine, nx + step, x_peer).wait_send()

    @pl.loop(0, chunks)
    def _(c):
        part_copy(c).wait_send()
        for n in range(3):
            hid_copy(hid_block(c, gy, gz), c * 3 + n, hid_targets[n]).wait_send()

    @pl.loop(0, out_chunks)
    def _(n):
        @pl.loop(1, nx)
        def _(step):
            term_copy(n, step).wait_send()

    @pl.loop(1, devices)
    def _(step):
        score_copy(lax.rem(own + step, devices), step).wait_recv()

    total = score_buf[0]
    for slot in range(1, devices):
        total = total + score_buf[slot]
    score_ref[...] = total

    @pl.loop(1, devices)
    def _(step):
        score_copy(own, step).wait_send()


def fused_local(nx, tokens, gate_weight, up_weight, down_weight, reward_weight, candidate_ids):
    rows, width = tokens.shape
    units = gate_weight.shape[1]
    depth, out_width = down_weight.shape
    total_rows = rows * nx * 2
    pieces = 4
    chunks, out_chunks = units // WIDE, out_width // OUT_WIDE
    devices = nx * 4
    following = jnp.concatenate([candidate_ids[1:], jnp.full((1,), -1, jnp.int32)])
    last_ids = jnp.where(candidate_ids != following, candidate_ids, -1).reshape(1, total_rows)
    reward = reward_weight.astype(jnp.float32).reshape(1, out_width)
    vmem, hbm = pl.BlockSpec(memory_space=pltpu.VMEM), pl.BlockSpec(memory_space=pl.ANY)
    bf, f32, dma = jnp.bfloat16, jnp.float32, pltpu.SemaphoreType.DMA
    term_shape = (out_chunks, nx, 4 * rows, OUT_WIDE // 2)
    mixed, scores = pl.pallas_call(
        lambda *refs: fused_kernel((nx, rows, pieces, chunks, out_chunks), *refs),
        out_shape=(
            jax.ShapeDtypeStruct((2 * rows, out_width), bf),
            jax.ShapeDtypeStruct((CANDS, 128), f32),
        ),
        in_specs=[vmem, hbm, hbm, hbm, vmem, vmem],
        out_specs=(vmem, vmem),
        scratch_shapes=[
            pltpu.VMEM((rows * pieces, width // pieces), f32),
            pltpu.VMEM((total_rows, width), f32),
            pltpu.VMEM((total_rows, width), bf),
            pltpu.VMEM((nx * 2, rows * pieces, width // pieces), bf),
            pltpu.VMEM((chunks, width, WIDE), bf),
            pltpu.VMEM((chunks, width, WIDE), bf),
            pltpu.VMEM((out_chunks, depth, OUT_WIDE), bf),
            pltpu.VMEM((chunks, 2, 2 * total_rows, WIDE // 2), bf),
            pltpu.VMEM((chunks, 2 * total_rows, WIDE // 2), bf),
            pltpu.VMEM((total_rows, depth), bf),
            pltpu.VMEM(term_shape, bf),
            pltpu.VMEM(term_shape, bf),
            pltpu.VMEM((devices, CANDS, 128), f32),
            dma((chunks,)), dma((chunks,)), dma((out_chunks,)),
            dma((nx * 2,)), dma((nx * 2,)),
            dma((chunks,)), dma((chunks,)),
            dma((chunks * 3,)), dma((chunks * 4,)),
            dma((out_chunks, nx)), dma((out_chunks, nx)),
            dma((devices,)), dma((devices,)),
        ],
        compiler_params=pltpu.CompilerParams(
            collective_id=0, has_side_effects=True, vmem_limit_bytes=VMEM_BYTES
        ),
        cost_estimate=pl.CostEstimate(
            flops=2 * total_rows * (2 * width * units + depth * out_width),
            bytes_accessed=2 * (2 * width * units + depth * out_width), transcendentals=0,
        ),
    )(tokens, gate_weight, up_weight, down_weight, reward, last_ids)
    return mixed, scores[:, 0]


def fits_fused(mesh, tokens, gate_weight, down_weight):
    nx, ny, nz = mesh.shape["gx"], mesh.shape["gy"], mesh.shape["gz"]
    if ny != 2 or nz != 2:
        return False
    rows, units = tokens.shape[0] // (mesh.shape["groups"] * nx * ny), gate_weight.shape[1] // (nx * ny)
    out_width = down_weight.shape[1] // (ny * nz)
    weights = 2 * (2 * units * gate_weight.shape[0] // nz + ny * units * out_width)
    return (
        rows % 4 == 0 and (rows * 2 * nx) % 16 == 0 and units % WIDE == 0 and out_width % OUT_WIDE == 0
        and weights < 48 * 1024 * 1024 and rows * nx * ny <= 128
    )


def solution(mesh):
    def call(tokens, gate_weight, up_weight, down_weight, reward_weight, candidate_ids):
        fused = fits_fused(mesh, tokens, gate_weight, down_weight)
        local = (lambda *blocks: fused_local(mesh.shape["gx"], *blocks)) if fused else plain_local
        return placed_call(mesh, local)(
            tokens, gate_weight, up_weight, down_weight, reward_weight, candidate_ids
        )

    return call


def placed_call(mesh, local):
    placed = (
        P(("groups", "gx", "gy"), "gz"),
        P("gz", ("gx", "gy")),
        P("gz", ("gx", "gy")),
        P("gx", ("gy", "gz")),
        P(("gy", "gz")),
        P("groups"),
    )
    return jax.shard_map(
        local,
        mesh=mesh,
        in_specs=placed,
        out_specs=(P(("groups", "gx"), ("gy", "gz")), P("groups")),
        check_vma=False,
    )
```

```python
import jax
import jax.numpy as jnp
from jax import lax
from jax.experimental import pallas as pl
from jax.experimental.pallas import tpu as pltpu
from jax.sharding import PartitionSpec as P

CANDS = 16


def swiglu_pair(summed, unit_count):
    row_count = summed.shape[0]
    split_pair = summed.reshape(row_count, -1, 2, unit_count)
    gate_part = split_pair[:, :, 0, :].reshape(row_count, -1)
    upper_part = split_pair[:, :, 1, :].reshape(row_count, -1)
    return (jax.nn.silu(gate_part) * upper_part).astype(jnp.bfloat16)


def combine_pairs(partial_value, unit_count):
    summed = lax.psum(partial_value.astype(jnp.bfloat16), "gz").astype(jnp.float32)
    return swiglu_pair(summed, unit_count)


def plain_local(tokens, gate_weight, up_weight, down_weight, reward_weight, candidate_ids):
    unit_count = gate_weight.shape[1]
    paired = jnp.concatenate([gate_weight, up_weight], axis=1)
    local_rows = tokens.shape[0]
    gy_count = lax.axis_size("gy")
    out_rows = local_rows * gy_count
    all_tokens = lax.all_gather(tokens, ("gx", "gy"), axis=0, tiled=True)
    partial_value = jnp.dot(all_tokens, paired, preferred_element_type=jnp.float32)
    hidden_part = combine_pairs(partial_value, unit_count)
    hidden_all = lax.all_gather(hidden_part, "gy", axis=1, tiled=True)
    summed_out = lax.psum_scatter(
        jnp.dot(hidden_all, down_weight, preferred_element_type=jnp.float32).astype(jnp.bfloat16),
        "gx",
        scatter_dimension=0,
        tiled=True,
    )
    values = jnp.dot(summed_out, reward_weight, preferred_element_type=jnp.float32)
    first_row = lax.axis_index("gx") * out_rows
    extended = jnp.concatenate([candidate_ids, jnp.full((1,), -1, jnp.int32)])
    own_ids = lax.dynamic_slice_in_dim(extended, first_row, out_rows, 0)
    next_ids = lax.dynamic_slice_in_dim(extended, first_row + 1, out_rows, 0)
    matches = (own_ids[:, None] == jnp.arange(CANDS, dtype=jnp.int32)[None, :]) & (
        own_ids != next_ids
    )[:, None]
    partial_scores = jnp.sum(
        jnp.where(matches, values[:, None], jnp.zeros_like(values)[:, None]), axis=0
    )
    scores = lax.psum(partial_scores, ("gx", "gy", "gz"))
    return (summed_out, scores)


MESH = pl.DeviceIdType.MESH
WIDE = 256
OUT_WIDE = 512
PIECES = 2
GROUP = 2
SUBS = 4
VMEM_BYTES = 60 * 1024 * 1024


def fused_kernel(
    sizes, tok_ref, gate_ref, up_ref, down_ref, reward_ref, ids_ref, out_ref, score_ref,
    tok_f32, x_f32, x_bf, blocks, gate_buf, up_buf, down_buf, part, part_in, hid, term, term_in, score_buf, sums,
    gate_sem, up_sem, down_sem, tok_send, tok_recv, part_send, part_recv, hid_send, hid_recv,
    term_send, term_recv, score_send, score_recv,
):
    nx, rows, pieces, chunks, out_chunks = sizes
    cut = tok_ref.shape[1] // pieces
    sub = cut // SUBS
    out_rows = 2 * rows
    total_rows = x_bf.shape[0]
    half = WIDE // 2
    out_half = OUT_WIDE // 2
    group, gx, gy, gz = (lax.axis_index(a) for a in ("groups", "gx", "gy", "gz"))
    gy_other, gz_other = 1 - gy, 1 - gz
    z_peers = [(group, lax.rem(gx + step, nx), gy, gz) for step in range(1, nx)]
    near_peers = [(group, gx, gy_other, gz), (group, gx, gy_other, gz_other), (group, gx, gy, gz_other)]
    near_slots = [gy_other * 2 + gz, gy_other * 2 + gz_other, gy * 2 + gz_other]
    own = gy * 2 + gz

    def row_copy(source, target, sem, p):
        return pltpu.make_async_copy(source.at[pl.ds(pl.multiple_of(p * cut, cut), cut)], target.at[p], sem.at[p])

    def down_copy(n):
        cols = pl.ds(pl.multiple_of(n * OUT_WIDE, OUT_WIDE), OUT_WIDE)
        return pltpu.make_async_copy(down_ref.at[:, cols], down_buf.at[n], down_sem.at[n])

    @pl.loop(0, pieces)
    def _(p):
        row_copy(gate_ref, gate_buf, gate_sem, p).start()
        row_copy(up_ref, up_buf, up_sem, p).start()

    @pl.loop(0, out_chunks)
    def _(n):
        down_copy(n).start()

    barrier = pltpu.get_barrier_semaphore()

    for target in z_peers + near_peers:
        pl.semaphore_signal(barrier, inc=1, device_id=target, device_id_type=MESH)

    mine = gx * 2 + gy
    for p in range(pieces):
        for q in range(SUBS):
            tok_f32[p, pl.ds(q * rows, rows), :] = tok_ref[:, pl.ds(p * cut + q * sub, sub)].astype(jnp.float32)
        blocks[p, mine] = tok_f32[p].astype(jnp.bfloat16)
    pl.semaphore_wait(barrier, nx + 2)

    def tok_copy(p, slot, send, target):
        return pltpu.make_async_remote_copy(
            src_ref=blocks.at[p, slot], dst_ref=blocks.at[p, slot], send_sem=tok_send.at[p, send],
            recv_sem=tok_recv.at[p, slot], device_id=target, device_id_type=MESH,
        )

    x_peer = (group, gx, gy_other, gz)

    @pl.loop(0, pieces)
    def _(p):
        tok_copy(p, mine, 0, x_peer).start()

        @pl.loop(1, nx)
        def _(step):
            tok_copy(p, mine, step, (group, lax.rem(gx + step, nx), gy, gz)).start()

    def forward(p):
        @pl.loop(1, nx)
        def _(step):
            slot = lax.rem(gx + nx - step, nx) * 2 + gy
            tok_copy(p, slot, 0, x_peer).wait_recv()
            tok_copy(p, slot, nx + step, x_peer).start()

    spans = [(c, min(c + GROUP, chunks)) for c in range(0, chunks, GROUP)]
    half_units = chunks * half
    core_peer = (group, gx, gy, gz_other)
    across = gy_other * 2 + gz

    def part_copy(g):
        first, end = spans[g]
        return pltpu.make_async_remote_copy(
            src_ref=part.at[gz_other, pl.ds(first, end - first)], dst_ref=part_in.at[pl.ds(first, end - first)],
            send_sem=part_send.at[g], recv_sem=part_recv.at[g],
            device_id=(group, gx, gy, gz_other), device_id_type=MESH,
        )

    def hid_copy(g, slot, send, target):
        first, end = spans[g]
        cols = hid.at[:, pl.ds(pl.multiple_of(slot * half_units + first * half, half), (end - first) * half)]
        return pltpu.make_async_remote_copy(
            src_ref=cols, dst_ref=cols, send_sem=hid_send.at[g, send],
            recv_sem=hid_recv.at[g, slot], device_id=target, device_id_type=MESH,
        )

    def finish(g):
        part_copy(g).wait_recv()

        @pl.loop(*spans[g])
        def _(c):
            gate, up = (
                part[gz, c, pl.ds(n * total_rows, total_rows), :].astype(jnp.float32)
                + part_in[c, pl.ds(n * total_rows, total_rows), :].astype(jnp.float32)
                for n in range(2)
            )
            cols = pl.ds(pl.multiple_of(own * half_units + c * half, half), half)
            hid[:, cols] = (jax.nn.silu(gate) * up).astype(jnp.bfloat16)

        hid_copy(g, own, 0, x_peer).start()
        hid_copy(g, own, 1, core_peer).start()

    forward(0)
    for p in range(pieces):
        if p + 1 < pieces:
            forward(p + 1)

        @pl.loop(0, nx)
        def _(step):
            slot = lax.rem(gx + nx - step, nx) * 2 + gy_other
            tok_copy(p, slot, 0, x_peer).wait_recv()

        for d in range(nx * 2):
            tok_f32[p] = blocks[p, d].astype(jnp.float32)
            for q in range(SUBS):
                x_f32[pl.ds(d * rows, rows), pl.ds(q * sub, sub)] = tok_f32[p, pl.ds(q * rows, rows), :]
        x_bf[...] = x_f32[...].astype(jnp.bfloat16)
        row_copy(gate_ref, gate_buf, gate_sem, p).wait()
        row_copy(up_ref, up_buf, up_sem, p).wait()

        def multiply(start, end):
            @pl.loop(start, end)
            def _(c):
                x = x_bf[...]
                low = pl.ds(pl.multiple_of(c * half, half), half)
                high = pl.ds(pl.multiple_of(half_units + c * half, half), half)
                for n, weight in enumerate((gate_buf, up_buf)):
                    both = jnp.concatenate([weight[p, :, low], weight[p, :, high]], axis=1)
                    product = jnp.dot(x, both, preferred_element_type=jnp.float32)
                    if p > 0:
                        product = product + sums[c, n]
                    if p + 1 < pieces:
                        sums[c, n] = product
                    else:
                        product = product.astype(jnp.bfloat16)
                        for z in range(2):
                            part[z, c, pl.ds(n * total_rows, total_rows), :] = product[:, z * half:(z + 1) * half]

        if p + 1 < pieces:
            multiply(0, chunks)
        else:
            for g, span in enumerate(spans):
                multiply(*span)
                part_copy(g).start()
                if g > 0:
                    finish(g - 1)

    finish(len(spans) - 1)
    for g in range(len(spans)):
        hid_copy(g, across, 0, x_peer).wait_recv()
        hid_copy(g, across, 2, core_peer).start()
    for g in range(len(spans)):
        hid_copy(g, gy * 2 + gz_other, 1, core_peer).wait_recv()
        hid_copy(g, gy_other * 2 + gz_other, 2, core_peer).wait_recv()

    def term_copy(n, step):
        to = lax.rem(gx + step, nx)
        return pltpu.make_async_remote_copy(
            src_ref=term.at[n, to], dst_ref=term_in.at[n, gx], send_sem=term_send.at[n, step],
            recv_sem=term_recv.at[n, gx], device_id=(group, to, gy, gz), device_id_type=MESH,
        )

    def term_arrival(n, step):
        sender = lax.rem(gx + nx - step, nx)
        return sender, pltpu.make_async_remote_copy(
            src_ref=term.at[n, sender], dst_ref=term_in.at[n, sender], send_sem=term_send.at[n, step],
            recv_sem=term_recv.at[n, sender], device_id=(group, sender, gy, gz), device_id_type=MESH,
        )

    @pl.loop(0, out_chunks)
    def _(n):
        down_copy(n).wait()
        product = jnp.dot(hid[...], down_buf[n], preferred_element_type=jnp.float32)
        for to in range(nx):
            block = product[to * out_rows:(to + 1) * out_rows, :]
            term[n, to] = jnp.concatenate([block[:, :out_half], block[:, out_half:]], axis=0).astype(jnp.bfloat16)

        @pl.loop(1, nx)
        def _(step):
            term_copy(n, step).start()

    values = jnp.zeros((out_rows, 1), jnp.float32)
    reward = reward_ref[...].astype(jnp.float32)
    for n in range(out_chunks):
        summed = term[n, gx].astype(jnp.float32)
        for step in range(1, nx):
            sender, arrival = term_arrival(n, step)
            arrival.wait_recv()
            summed = summed + term_in[n, sender].astype(jnp.float32)
        for h in range(2):
            cols = pl.ds(n * OUT_WIDE + h * out_half, out_half)
            mixed = summed[h * out_rows:(h + 1) * out_rows, :].astype(jnp.bfloat16)
            out_ref[:, cols] = mixed
            for q in range(out_half // 128):
                line = (n * OUT_WIDE + h * out_half) // 128 + q
                scaled = mixed[:, q * 128:(q + 1) * 128].astype(jnp.float32) * reward[line:line + 1, :]
                values = values + jnp.sum(scaled, axis=1, keepdims=True)

    spread = jnp.concatenate([jnp.where(gx == j, values, jnp.zeros_like(values)) for j in range(nx)], axis=0)
    spread = jnp.broadcast_to(spread, (total_rows, 128))
    place = lax.broadcasted_iota(jnp.int32, (CANDS, total_rows), 1)
    same = ids_ref[...] == lax.broadcasted_iota(jnp.int32, (CANDS, total_rows), 0)
    last = jnp.max(jnp.where(same, place, -1), axis=1, keepdims=True)
    matches = (place == last).astype(jnp.float32)
    score_buf[own] = jnp.dot(matches, spread, preferred_element_type=jnp.float32, precision=lax.Precision.HIGHEST)

    def score_copy(slot, send, target):
        return pltpu.make_async_remote_copy(
            src_ref=score_buf.at[slot], dst_ref=score_buf.at[slot], send_sem=score_send.at[send],
            recv_sem=score_recv.at[slot], device_id=target, device_id_type=MESH,
        )

    for n, target in enumerate(near_peers):
        score_copy(own, n, target).start()

    for slot, target in zip(near_slots, near_peers):
        score_copy(slot, 0, target).wait_recv()
    score_buf[4 + gx] = (score_buf[0] + score_buf[1]) + (score_buf[2] + score_buf[3])
    for n, target in enumerate(z_peers):
        score_copy(4 + gx, 3 + n, target).start()
    for step in range(1, nx):
        score_copy(4 + lax.rem(gx + step, nx), 0, z_peers[step - 1]).wait_recv()
    total = score_buf[4]
    for j in range(1, nx):
        total = total + score_buf[4 + j]
    diagonal = lax.broadcasted_iota(jnp.int32, (CANDS, 128), 0) == lax.broadcasted_iota(jnp.int32, (CANDS, 128), 1)
    score_ref[...] = jnp.sum(jnp.where(diagonal, total, 0.0), axis=0, keepdims=True)[:, :CANDS]


    @pl.loop(0, pieces)
    def _(p):
        @pl.loop(0, nx)
        def _(step):
            tok_copy(p, mine, step, x_peer).wait_send()

        @pl.loop(1, nx)
        def _(step):
            tok_copy(p, mine, nx + step, x_peer).wait_send()

    for g in range(len(spans)):
        part_copy(g).wait_send()
        hid_copy(g, own, 0, x_peer).wait_send()
        hid_copy(g, own, 1, core_peer).wait_send()
        hid_copy(g, across, 2, core_peer).wait_send()

    @pl.loop(0, out_chunks)
    def _(n):
        @pl.loop(1, nx)
        def _(step):
            term_copy(n, step).wait_send()

    for n, target in enumerate(near_peers):
        score_copy(own, n, target).wait_send()
    for n, target in enumerate(z_peers):
        score_copy(4 + gx, 3 + n, target).wait_send()


def fused_local(nx, tokens, gate_weight, up_weight, down_weight, reward_weight, candidate_ids):
    rows, width = tokens.shape
    units = gate_weight.shape[1]
    depth, out_width = down_weight.shape
    total_rows = rows * nx * 2
    pieces, cut = PIECES, width // PIECES
    chunks, out_chunks = units // WIDE, out_width // OUT_WIDE
    groups = pl.cdiv(chunks, GROUP)
    ids = candidate_ids.reshape(1, total_rows)
    reward = reward_weight.reshape(out_width // 128, 128)
    vmem, hbm = pl.BlockSpec(memory_space=pltpu.VMEM), pl.BlockSpec(memory_space=pl.ANY)
    bf, f32, dma = jnp.bfloat16, jnp.float32, pltpu.SemaphoreType.DMA
    term_shape = (out_chunks, nx, 4 * rows, OUT_WIDE // 2)
    mixed, scores = pl.pallas_call(
        lambda *refs: fused_kernel((nx, rows, pieces, chunks, out_chunks), *refs),
        out_shape=(
            jax.ShapeDtypeStruct((2 * rows, out_width), bf),
            jax.ShapeDtypeStruct((1, CANDS), f32),
        ),
        in_specs=[vmem, hbm, hbm, hbm, vmem, vmem],
        out_specs=(vmem, vmem),
        scratch_shapes=[
            pltpu.VMEM((pieces, rows * SUBS, cut // SUBS), f32),
            pltpu.VMEM((total_rows, cut), f32),
            pltpu.VMEM((total_rows, cut), bf),
            pltpu.VMEM((pieces, nx * 2, rows * SUBS, cut // SUBS), bf),
            pltpu.VMEM((pieces, cut, units), bf),
            pltpu.VMEM((pieces, cut, units), bf),
            pltpu.VMEM((out_chunks, depth, OUT_WIDE), bf),
            pltpu.VMEM((2, chunks, 2 * total_rows, WIDE // 2), bf),
            pltpu.VMEM((chunks, 2 * total_rows, WIDE // 2), bf),
            pltpu.VMEM((total_rows, depth), bf),
            pltpu.VMEM(term_shape, bf),
            pltpu.VMEM(term_shape, bf),
            pltpu.VMEM((4 + nx, CANDS, 128), f32),
            pltpu.VMEM((chunks, 2, total_rows, WIDE), f32),
            dma((pieces,)), dma((pieces,)), dma((out_chunks,)),
            dma((pieces, nx * 2)), dma((pieces, nx * 2)),
            dma((groups,)), dma((groups,)),
            dma((groups, 3)), dma((groups, 4)),
            dma((out_chunks, nx)), dma((out_chunks, nx)),
            dma((4 + nx,)), dma((4 + nx,)),
        ],
        compiler_params=pltpu.CompilerParams(
            collective_id=0, has_side_effects=True, vmem_limit_bytes=VMEM_BYTES
        ),
        cost_estimate=pl.CostEstimate(
            flops=2 * total_rows * (2 * width * units + depth * out_width),
            bytes_accessed=2 * (2 * width * units + depth * out_width), transcendentals=0,
        ),
    )(tokens, gate_weight, up_weight, down_weight, reward, ids)
    return mixed, scores.reshape(CANDS)


def fits_fused(mesh, tokens, gate_weight, down_weight):
    nx, ny, nz = mesh.shape["gx"], mesh.shape["gy"], mesh.shape["gz"]
    if ny != 2 or nz != 2:
        return False
    rows, units = tokens.shape[0] // (mesh.shape["groups"] * nx * ny), gate_weight.shape[1] // (nx * ny)
    out_width = down_weight.shape[1] // (ny * nz)
    weights = 2 * (2 * units * gate_weight.shape[0] // nz + ny * units * out_width)
    return (
        rows % 4 == 0 and gate_weight.shape[0] % (2048 * nz) == 0 and (rows * 2 * nx) % 16 == 0 and units % WIDE == 0 and out_width % OUT_WIDE == 0
        and weights < 48 * 1024 * 1024 and rows * nx * ny <= 128
    )


def solution(mesh):
    def call(tokens, gate_weight, up_weight, down_weight, reward_weight, candidate_ids):
        fused = fits_fused(mesh, tokens, gate_weight, down_weight)
        local = (lambda *blocks: fused_local(mesh.shape["gx"], *blocks)) if fused else plain_local
        return placed_call(mesh, local)(
            tokens, gate_weight, up_weight, down_weight, reward_weight, candidate_ids
        )

    return call


def placed_call(mesh, local):
    placed = (
        P(("groups", "gx", "gy"), "gz"),
        P("gz", ("gx", "gy")),
        P("gz", ("gx", "gy")),
        P("gx", ("gy", "gz")),
        P(("gy", "gz")),
        P("groups"),
    )
    return jax.shard_map(
        local,
        mesh=mesh,
        in_specs=placed,
        out_specs=(P(("groups", "gx"), ("gy", "gz")), P("groups")),
        check_vma=False,
    )
```

```python
import jax
import jax.numpy as jnp
from jax import lax
from jax.experimental import pallas as pl
from jax.experimental.pallas import tpu as pltpu
from jax.sharding import PartitionSpec as P

CANDS = 16


def swiglu_pair(summed, unit_count):
    row_count = summed.shape[0]
    split_pair = summed.reshape(row_count, -1, 2, unit_count)
    gate_part = split_pair[:, :, 0, :].reshape(row_count, -1)
    upper_part = split_pair[:, :, 1, :].reshape(row_count, -1)
    return (jax.nn.silu(gate_part) * upper_part).astype(jnp.bfloat16)


def combine_pairs(partial_value, unit_count):
    summed = lax.psum(partial_value.astype(jnp.bfloat16), "gz").astype(jnp.float32)
    return swiglu_pair(summed, unit_count)


def plain_local(tokens, gate_weight, up_weight, down_weight, reward_weight, candidate_ids):
    unit_count = gate_weight.shape[1]
    paired = jnp.concatenate([gate_weight, up_weight], axis=1)
    local_rows = tokens.shape[0]
    gy_count = lax.axis_size("gy")
    out_rows = local_rows * gy_count
    all_tokens = lax.all_gather(tokens, ("gx", "gy"), axis=0, tiled=True)
    partial_value = jnp.dot(all_tokens, paired, preferred_element_type=jnp.float32)
    hidden_part = combine_pairs(partial_value, unit_count)
    hidden_all = lax.all_gather(hidden_part, "gy", axis=1, tiled=True)
    summed_out = lax.psum_scatter(
        jnp.dot(hidden_all, down_weight, preferred_element_type=jnp.float32).astype(jnp.bfloat16),
        "gx",
        scatter_dimension=0,
        tiled=True,
    )
    values = jnp.dot(summed_out, reward_weight, preferred_element_type=jnp.float32)
    first_row = lax.axis_index("gx") * out_rows
    extended = jnp.concatenate([candidate_ids, jnp.full((1,), -1, jnp.int32)])
    own_ids = lax.dynamic_slice_in_dim(extended, first_row, out_rows, 0)
    next_ids = lax.dynamic_slice_in_dim(extended, first_row + 1, out_rows, 0)
    matches = (own_ids[:, None] == jnp.arange(CANDS, dtype=jnp.int32)[None, :]) & (
        own_ids != next_ids
    )[:, None]
    partial_scores = jnp.sum(
        jnp.where(matches, values[:, None], jnp.zeros_like(values)[:, None]), axis=0
    )
    scores = lax.psum(partial_scores, ("gx", "gy", "gz"))
    return (summed_out, scores)


MESH = pl.DeviceIdType.MESH
WIDE = 256
OUT_WIDE = 256
PIECES = 2
GROUP = 2
SUBS = 4
VMEM_BYTES = 60 * 1024 * 1024


def fused_kernel(
    sizes, tok_ref, gate_ref, up_ref, down_ref, reward_ref, ids_ref, out_ref, score_ref,
    tok_f32, x_f32, x_bf, blocks, gate_buf, up_buf, down_buf, part, part_in, hid, term, term_in, score_buf, sums,
    gate_sem, up_sem, down_sem, tok_send, tok_recv, part_send, part_recv, hid_send, hid_recv,
    term_send, term_recv, score_send, score_recv,
):
    nx, rows, pieces, chunks, out_chunks = sizes
    cut = tok_ref.shape[1] // pieces
    sub = cut // SUBS
    out_rows = 2 * rows
    total_rows = x_bf.shape[0]
    half = WIDE // 2
    out_half = OUT_WIDE // 2
    group, gx, gy, gz = (lax.axis_index(a) for a in ("groups", "gx", "gy", "gz"))
    gy_other, gz_other = 1 - gy, 1 - gz
    z_peers = [(group, lax.rem(gx + step, nx), gy, gz) for step in range(1, nx)]
    near_peers = [(group, gx, gy_other, gz), (group, gx, gy_other, gz_other), (group, gx, gy, gz_other)]
    near_slots = [gy_other * 2 + gz, gy_other * 2 + gz_other, gy * 2 + gz_other]
    own = gy * 2 + gz

    def row_copy(source, target, sem, p):
        return pltpu.make_async_copy(source.at[pl.ds(pl.multiple_of(p * cut, cut), cut)], target.at[p], sem.at[p])

    def down_copy(n):
        cols = pl.ds(pl.multiple_of(n * OUT_WIDE, OUT_WIDE), OUT_WIDE)
        return pltpu.make_async_copy(down_ref.at[:, cols], down_buf.at[n], down_sem.at[n])

    @pl.loop(0, pieces)
    def _(p):
        row_copy(gate_ref, gate_buf, gate_sem, p).start()
        row_copy(up_ref, up_buf, up_sem, p).start()

    @pl.loop(0, out_chunks)
    def _(n):
        down_copy(n).start()

    barrier = pltpu.get_barrier_semaphore()

    for target in z_peers + near_peers:
        pl.semaphore_signal(barrier, inc=1, device_id=target, device_id_type=MESH)

    mine = gx * 2 + gy
    for p in range(pieces):
        for q in range(SUBS):
            tok_f32[p, pl.ds(q * rows, rows), :] = tok_ref[:, pl.ds(p * cut + q * sub, sub)].astype(jnp.float32)
        blocks[p, mine] = tok_f32[p].astype(jnp.bfloat16)
    pl.semaphore_wait(barrier, nx + 2)

    def tok_copy(p, slot, send, target):
        return pltpu.make_async_remote_copy(
            src_ref=blocks.at[p, slot], dst_ref=blocks.at[p, slot], send_sem=tok_send.at[p, send],
            recv_sem=tok_recv.at[p, slot], device_id=target, device_id_type=MESH,
        )

    x_peer = (group, gx, gy_other, gz)

    @pl.loop(0, pieces)
    def _(p):
        tok_copy(p, mine, 0, x_peer).start()

        @pl.loop(1, nx)
        def _(step):
            tok_copy(p, mine, step, (group, lax.rem(gx + step, nx), gy, gz)).start()

    def forward(p):
        @pl.loop(1, nx)
        def _(step):
            slot = lax.rem(gx + nx - step, nx) * 2 + gy
            tok_copy(p, slot, 0, x_peer).wait_recv()
            tok_copy(p, slot, nx + step, x_peer).start()

    spans = [(c, min(c + GROUP, chunks)) for c in range(0, chunks, GROUP)]
    half_units = chunks * half
    core_peer = (group, gx, gy, gz_other)
    across = gy_other * 2 + gz

    def part_copy(g):
        first, end = spans[g]
        return pltpu.make_async_remote_copy(
            src_ref=part.at[gz_other, pl.ds(first, end - first)], dst_ref=part_in.at[pl.ds(first, end - first)],
            send_sem=part_send.at[g], recv_sem=part_recv.at[g],
            device_id=(group, gx, gy, gz_other), device_id_type=MESH,
        )

    def hid_copy(g, slot, send, target):
        first, end = spans[g]
        cols = hid.at[:, pl.ds(pl.multiple_of(slot * half_units + first * half, half), (end - first) * half)]
        return pltpu.make_async_remote_copy(
            src_ref=cols, dst_ref=cols, send_sem=hid_send.at[g, send],
            recv_sem=hid_recv.at[g, slot], device_id=target, device_id_type=MESH,
        )

    def finish(g):
        part_copy(g).wait_recv()

        @pl.loop(*spans[g])
        def _(c):
            gate, up = (
                part[gz, c, pl.ds(n * total_rows, total_rows), :].astype(jnp.float32)
                + part_in[c, pl.ds(n * total_rows, total_rows), :].astype(jnp.float32)
                for n in range(2)
            )
            cols = pl.ds(pl.multiple_of(own * half_units + c * half, half), half)
            hid[:, cols] = (jax.nn.silu(gate) * up).astype(jnp.bfloat16)

        hid_copy(g, own, 0, x_peer).start()
        hid_copy(g, own, 1, core_peer).start()

    forward(0)
    for p in range(pieces):
        if p + 1 < pieces:
            forward(p + 1)

        @pl.loop(0, nx)
        def _(step):
            slot = lax.rem(gx + nx - step, nx) * 2 + gy_other
            tok_copy(p, slot, 0, x_peer).wait_recv()

        for d in range(nx * 2):
            tok_f32[p] = blocks[p, d].astype(jnp.float32)
            for q in range(SUBS):
                x_f32[pl.ds(d * rows, rows), pl.ds(q * sub, sub)] = tok_f32[p, pl.ds(q * rows, rows), :]
        x_bf[...] = x_f32[...].astype(jnp.bfloat16)
        row_copy(gate_ref, gate_buf, gate_sem, p).wait()
        row_copy(up_ref, up_buf, up_sem, p).wait()

        def multiply(start, end):
            @pl.loop(start, end)
            def _(c):
                x = x_bf[...]
                low = pl.ds(pl.multiple_of(c * half, half), half)
                high = pl.ds(pl.multiple_of(half_units + c * half, half), half)
                for n, weight in enumerate((gate_buf, up_buf)):
                    both = jnp.concatenate([weight[p, :, low], weight[p, :, high]], axis=1)
                    product = jnp.dot(x, both, preferred_element_type=jnp.float32)
                    if p > 0:
                        product = product + sums[c, n]
                    if p + 1 < pieces:
                        sums[c, n] = product
                    else:
                        product = product.astype(jnp.bfloat16)
                        for z in range(2):
                            part[z, c, pl.ds(n * total_rows, total_rows), :] = product[:, z * half:(z + 1) * half]

        if p + 1 < pieces:
            multiply(0, chunks)
        else:
            for g, span in enumerate(spans):
                multiply(*span)
                part_copy(g).start()
                if g > 0:
                    finish(g - 1)

    finish(len(spans) - 1)
    for g in range(len(spans)):
        hid_copy(g, across, 0, x_peer).wait_recv()
        hid_copy(g, across, 2, core_peer).start()
    for g in range(len(spans)):
        hid_copy(g, gy * 2 + gz_other, 1, core_peer).wait_recv()
        hid_copy(g, gy_other * 2 + gz_other, 2, core_peer).wait_recv()

    def term_copy(n, step):
        to = lax.rem(gx + step, nx)
        return pltpu.make_async_remote_copy(
            src_ref=term.at[n, to], dst_ref=term_in.at[n, gx], send_sem=term_send.at[n, step],
            recv_sem=term_recv.at[n, gx], device_id=(group, to, gy, gz), device_id_type=MESH,
        )

    def term_arrival(n, step):
        sender = lax.rem(gx + nx - step, nx)
        return sender, pltpu.make_async_remote_copy(
            src_ref=term.at[n, sender], dst_ref=term_in.at[n, sender], send_sem=term_send.at[n, step],
            recv_sem=term_recv.at[n, sender], device_id=(group, sender, gy, gz), device_id_type=MESH,
        )

    @pl.loop(0, out_chunks)
    def _(n):
        down_copy(n).wait()
        product = jnp.dot(hid[...], down_buf[n], preferred_element_type=jnp.float32)
        for to in range(nx):
            block = product[to * out_rows:(to + 1) * out_rows, :]
            term[n, to] = jnp.concatenate([block[:, :out_half], block[:, out_half:]], axis=0).astype(jnp.bfloat16)

        @pl.loop(1, nx)
        def _(step):
            term_copy(n, step).start()

    values = jnp.zeros((out_rows, 1), jnp.float32)
    reward = reward_ref[...].astype(jnp.float32)
    for n in range(out_chunks):
        summed = term[n, gx].astype(jnp.float32)
        for step in range(1, nx):
            sender, arrival = term_arrival(n, step)
            arrival.wait_recv()
            summed = summed + term_in[n, sender].astype(jnp.float32)
        for h in range(2):
            cols = pl.ds(n * OUT_WIDE + h * out_half, out_half)
            mixed = summed[h * out_rows:(h + 1) * out_rows, :].astype(jnp.bfloat16)
            out_ref[:, cols] = mixed
            for q in range(out_half // 128):
                line = (n * OUT_WIDE + h * out_half) // 128 + q
                scaled = mixed[:, q * 128:(q + 1) * 128].astype(jnp.float32) * reward[line:line + 1, :]
                values = values + jnp.sum(scaled, axis=1, keepdims=True)

    spread = jnp.concatenate([jnp.where(gx == j, values, jnp.zeros_like(values)) for j in range(nx)], axis=0)
    spread = jnp.broadcast_to(spread, (total_rows, 128))
    place = lax.broadcasted_iota(jnp.int32, (CANDS, total_rows), 1)
    same = ids_ref[...] == lax.broadcasted_iota(jnp.int32, (CANDS, total_rows), 0)
    last = jnp.max(jnp.where(same, place, -1), axis=1, keepdims=True)
    matches = (place == last).astype(jnp.float32)
    score_buf[own] = jnp.dot(matches, spread, preferred_element_type=jnp.float32, precision=lax.Precision.HIGHEST)

    def score_copy(slot, send, target):
        return pltpu.make_async_remote_copy(
            src_ref=score_buf.at[slot], dst_ref=score_buf.at[slot], send_sem=score_send.at[send],
            recv_sem=score_recv.at[slot], device_id=target, device_id_type=MESH,
        )

    for n, target in enumerate(near_peers):
        score_copy(own, n, target).start()

    for slot, target in zip(near_slots, near_peers):
        score_copy(slot, 0, target).wait_recv()
    score_buf[4 + gx] = (score_buf[0] + score_buf[1]) + (score_buf[2] + score_buf[3])
    for n, target in enumerate(z_peers):
        score_copy(4 + gx, 3 + n, target).start()
    for step in range(1, nx):
        score_copy(4 + lax.rem(gx + step, nx), 0, z_peers[step - 1]).wait_recv()
    total = score_buf[4]
    for j in range(1, nx):
        total = total + score_buf[4 + j]
    diagonal = lax.broadcasted_iota(jnp.int32, (CANDS, 128), 0) == lax.broadcasted_iota(jnp.int32, (CANDS, 128), 1)
    score_ref[...] = jnp.sum(jnp.where(diagonal, total, 0.0), axis=0, keepdims=True)[:, :CANDS]


    @pl.loop(0, pieces)
    def _(p):
        @pl.loop(0, nx)
        def _(step):
            tok_copy(p, mine, step, x_peer).wait_send()

        @pl.loop(1, nx)
        def _(step):
            tok_copy(p, mine, nx + step, x_peer).wait_send()

    for g in range(len(spans)):
        part_copy(g).wait_send()
        hid_copy(g, own, 0, x_peer).wait_send()
        hid_copy(g, own, 1, core_peer).wait_send()
        hid_copy(g, across, 2, core_peer).wait_send()

    @pl.loop(0, out_chunks)
    def _(n):
        @pl.loop(1, nx)
        def _(step):
            term_copy(n, step).wait_send()

    for n, target in enumerate(near_peers):
        score_copy(own, n, target).wait_send()
    for n, target in enumerate(z_peers):
        score_copy(4 + gx, 3 + n, target).wait_send()


def fused_local(nx, tokens, gate_weight, up_weight, down_weight, reward_weight, candidate_ids):
    rows, width = tokens.shape
    units = gate_weight.shape[1]
    depth, out_width = down_weight.shape
    total_rows = rows * nx * 2
    pieces, cut = PIECES, width // PIECES
    chunks, out_chunks = units // WIDE, out_width // OUT_WIDE
    groups = pl.cdiv(chunks, GROUP)
    ids = candidate_ids.reshape(1, total_rows)
    reward = reward_weight.reshape(out_width // 128, 128)
    vmem, hbm = pl.BlockSpec(memory_space=pltpu.VMEM), pl.BlockSpec(memory_space=pl.ANY)
    bf, f32, dma = jnp.bfloat16, jnp.float32, pltpu.SemaphoreType.DMA
    term_shape = (out_chunks, nx, 4 * rows, OUT_WIDE // 2)
    mixed, scores = pl.pallas_call(
        lambda *refs: fused_kernel((nx, rows, pieces, chunks, out_chunks), *refs),
        out_shape=(
            jax.ShapeDtypeStruct((2 * rows, out_width), bf),
            jax.ShapeDtypeStruct((1, CANDS), f32),
        ),
        in_specs=[vmem, hbm, hbm, hbm, vmem, vmem],
        out_specs=(vmem, vmem),
        scratch_shapes=[
            pltpu.VMEM((pieces, rows * SUBS, cut // SUBS), f32),
            pltpu.VMEM((total_rows, cut), f32),
            pltpu.VMEM((total_rows, cut), bf),
            pltpu.VMEM((pieces, nx * 2, rows * SUBS, cut // SUBS), bf),
            pltpu.VMEM((pieces, cut, units), bf),
            pltpu.VMEM((pieces, cut, units), bf),
            pltpu.VMEM((out_chunks, depth, OUT_WIDE), bf),
            pltpu.VMEM((2, chunks, 2 * total_rows, WIDE // 2), bf),
            pltpu.VMEM((chunks, 2 * total_rows, WIDE // 2), bf),
            pltpu.VMEM((total_rows, depth), bf),
            pltpu.VMEM(term_shape, bf),
            pltpu.VMEM(term_shape, bf),
            pltpu.VMEM((4 + nx, CANDS, 128), f32),
            pltpu.VMEM((chunks, 2, total_rows, WIDE), f32),
            dma((pieces,)), dma((pieces,)), dma((out_chunks,)),
            dma((pieces, nx * 2)), dma((pieces, nx * 2)),
            dma((groups,)), dma((groups,)),
            dma((groups, 3)), dma((groups, 4)),
            dma((out_chunks, nx)), dma((out_chunks, nx)),
            dma((4 + nx,)), dma((4 + nx,)),
        ],
        compiler_params=pltpu.CompilerParams(
            collective_id=0, has_side_effects=True, vmem_limit_bytes=VMEM_BYTES
        ),
        cost_estimate=pl.CostEstimate(
            flops=2 * total_rows * (2 * width * units + depth * out_width),
            bytes_accessed=2 * (2 * width * units + depth * out_width), transcendentals=0,
        ),
    )(tokens, gate_weight, up_weight, down_weight, reward, ids)
    return mixed, scores.reshape(CANDS)


def fits_fused(mesh, tokens, gate_weight, down_weight):
    nx, ny, nz = mesh.shape["gx"], mesh.shape["gy"], mesh.shape["gz"]
    if ny != 2 or nz != 2:
        return False
    rows, units = tokens.shape[0] // (mesh.shape["groups"] * nx * ny), gate_weight.shape[1] // (nx * ny)
    out_width = down_weight.shape[1] // (ny * nz)
    weights = 2 * (2 * units * gate_weight.shape[0] // nz + ny * units * out_width)
    return (
        rows % 4 == 0 and gate_weight.shape[0] % (2048 * nz) == 0 and (rows * 2 * nx) % 16 == 0 and units % WIDE == 0 and out_width % OUT_WIDE == 0
        and weights < 48 * 1024 * 1024 and rows * nx * ny <= 128
    )


def solution(mesh):
    def call(tokens, gate_weight, up_weight, down_weight, reward_weight, candidate_ids):
        fused = fits_fused(mesh, tokens, gate_weight, down_weight)
        local = (lambda *blocks: fused_local(mesh.shape["gx"], *blocks)) if fused else plain_local
        return placed_call(mesh, local)(
            tokens, gate_weight, up_weight, down_weight, reward_weight, candidate_ids
        )

    return call


def placed_call(mesh, local):
    placed = (
        P(("groups", "gx", "gy"), "gz"),
        P("gz", ("gx", "gy")),
        P("gz", ("gx", "gy")),
        P("gx", ("gy", "gz")),
        P(("gy", "gz")),
        P("groups"),
    )
    return jax.shard_map(
        local,
        mesh=mesh,
        in_specs=placed,
        out_specs=(P(("groups", "gx"), ("gy", "gz")), P("groups")),
        check_vma=False,
    )
```
